32 devices in a mesh: frame: 16 (over z, x, core), group: 2 (over y).
Axes of the slice: x: 2, y: 2, z: 4, core: 2. Of those that a mesh axis runs over, the one named last changes fastest.
Arguments:
- queries: bfloat16 [2048, 2048], P('frame', 'group'), may hold values from -6 to 6
- keys: bfloat16 [2048, 256], P('frame', 'group'), may hold values from -50 to 50
- values: bfloat16 [2048, 256], P('frame', 'group'), may hold values from -6 to 6
- q_gain: float32 [128], replicated, may hold values from 0.4 to 2.5
- frame_bounds: int32 [2, 2048], P(None, 'frame'), may hold values from 0 to 16, as said below
- output_weight: bfloat16 [2, 1024, 4096], P('group', 'frame'), may hold values from -0.25 to 0.25
- attn_gate: float32 [1], replicated, may hold values from 0.4 to 1.6
Outputs:
- projected: bfloat16 [2048, 4096], P('frame', 'group')
The draws below stay inside these ranges and needn't reach their ends.
Inputs may be any that keep to these rules, and one draw needn't show every extreme that they name: `frame_bounds`: row 0 is below row 1 for every text token.
All inputs are finite; a program needn't handle non-finite values.
Results may differ from the reference program's by a relative error of at most 0.008.
The reference program's roundings to bfloat16 on the way count: a program that leaves them out, or rounds other values in their place, can miss the bound.
Values may be sent and summed in bfloat16 or wider, within the bound.
A program may use at most 64 MiB of HBM per device.

```python
import math
import jax
import jax.numpy as jnp
from jax import lax

HEAD_WIDTH = 128
QUERY_PER_GROUP = 8
OUTPUT_FEATURES = 4096
V_DEV = 128
KEY_VALUE_HEADS = 2
QUERY_HEADS = 16
TEXT_TOKENS = 2048
VISUAL_TOKENS = 2048
NBLK = 16


def frame_limits(key):
    lower_block = jax.random.randint(jax.random.fold_in(key, 31), (TEXT_TOKENS,), 0, NBLK)
    span_count = jax.random.randint(jax.random.fold_in(key, 32), (TEXT_TOKENS,), 1, NBLK + 1)
    upper_block = jnp.minimum(lower_block + span_count, NBLK)
    lower_block = lower_block.at[0].set(0)
    upper_block = upper_block.at[0].set(NBLK)
    return (lower_block.astype(jnp.int32), upper_block.astype(jnp.int32))


def draw_frame_bounds(key, part):
    lower_block, upper_block = frame_limits(key)
    return jnp.stack([lower_block, upper_block]).astype(jnp.int32)


def row_scales(key):
    return jnp.exp(jax.random.uniform(jax.random.fold_in(key, 42), (VISUAL_TOKENS, 1), jnp.float32, math.log(2.5), math.log(3.0)))


def draw_keys(key, part):
    sampled_values = jnp.clip(jax.random.normal(jax.random.fold_in(key, 41), (VISUAL_TOKENS, KEY_VALUE_HEADS * HEAD_WIDTH), jnp.float32), -6.0, 6.0)
    result = sampled_values * row_scales(key)
    return result.astype(jnp.bfloat16)


def draw_queries(key, part):
    sampled_values = jnp.clip(jax.random.normal(jax.random.fold_in(key, 51), (TEXT_TOKENS, QUERY_HEADS * HEAD_WIDTH), jnp.float32), -6.0, 6.0)
    return sampled_values.astype(jnp.bfloat16)


def shard_levels(own_key, extent, cuts, smallest, high):
    def one(axis_at, shards_of):
        heights = jax.random.uniform(jax.random.fold_in(jax.random.fold_in(own_key, 6), axis_at), (shards_of,), jnp.float32, smallest / len(cuts), high / len(cuts))
        return jnp.repeat(jnp.exp(heights), extent[axis_at] // shards_of).reshape((-1,) + (1,) * (len(extent) - axis_at - 1))

    gain = one(*cuts[0])
    for cut in cuts[1:]:
        gain = gain * one(*cut)
    return gain


def normal_values(rng, extent, scale, bound, pieces=(), dtype=jnp.bfloat16):
    drawn = jax.random.normal(rng, extent, jnp.float32) * scale
    if len(pieces) > 0:
        drawn = shard_levels(rng, extent, pieces, -0.22, 0.18) * drawn
    return jnp.clip(drawn, min=-bound, max=bound).astype(dtype)


def setup_inputs(seed: int = 0) -> dict:
    streams_of = jax.random.split(jax.random.key(seed), 8)
    queries = draw_queries(jax.random.fold_in(streams_of[7], 71), 0)
    keys = draw_keys(jax.random.fold_in(streams_of[7], 71), 0)
    values = normal_values(streams_of[2], (VISUAL_TOKENS, KEY_VALUE_HEADS * HEAD_WIDTH), 1.0, 6.0, ((0, 16), (1, 2)))
    q_gain = jnp.clip(jnp.exp(jax.random.uniform(streams_of[3], (HEAD_WIDTH,), jnp.float32, math.log(0.4), math.log(2.5))), 0.4, 2.5)
    frame_bounds = draw_frame_bounds(jax.random.fold_in(streams_of[7], 71), 0)
    output_weight = normal_values(streams_of[5], (KEY_VALUE_HEADS, QUERY_PER_GROUP * HEAD_WIDTH, OUTPUT_FEATURES), 512 ** -0.5, 0.25, ((0, 2), (1, 16)))
    attn_gate = jnp.clip(jax.random.uniform(streams_of[6], (1,), jnp.float32, 0.4, 1.6), 0.4, 1.6)
    return dict(queries=queries, keys=keys, values=values, q_gain=q_gain, frame_bounds=frame_bounds, output_weight=output_weight, attn_gate=attn_gate)


def reference(queries, keys, values, q_gain, frame_bounds, output_weight, attn_gate):
    as_float = queries.astype(jnp.float32).reshape(TEXT_TOKENS, QUERY_HEADS, HEAD_WIDTH)
    normalized_input = as_float * lax.rsqrt(lax.optimization_barrier(jnp.mean(as_float * as_float, axis=-1, keepdims=True)) + 1e-05) * q_gain
    normalized_input = normalized_input.astype(jnp.bfloat16).reshape(TEXT_TOKENS, KEY_VALUE_HEADS, QUERY_PER_GROUP * HEAD_WIDTH)
    text_block = math.gcd(TEXT_TOKENS, 512)
    block_count = TEXT_TOKENS // text_block
    lower_rows = frame_bounds[0].reshape(block_count, text_block)
    upper_rows = frame_bounds[1].reshape(block_count, text_block)
    score_scale = 1.0 / math.sqrt(HEAD_WIDTH)
    block_ids = (jnp.arange(VISUAL_TOKENS) // V_DEV).astype(jnp.int32)

    def single_head(head_index):
        head_keys = lax.dynamic_slice_in_dim(keys, head_index * HEAD_WIDTH, HEAD_WIDTH, 1)
        head_values = lax.dynamic_slice_in_dim(values, head_index * HEAD_WIDTH, HEAD_WIDTH, 1)
        head_queries = lax.dynamic_index_in_dim(normalized_input, head_index, 1, keepdims=False)
        head_queries = head_queries.reshape(block_count, text_block * QUERY_PER_GROUP, HEAD_WIDTH)

        def one_block(packed):
            query_rows, lower_bound, upper_bound = packed
            scores = jnp.dot(query_rows, head_keys.T, preferred_element_type=jnp.float32) * score_scale
            lower_here = jnp.repeat(lower_bound, QUERY_PER_GROUP)[:, None]
            upper_here = jnp.repeat(upper_bound, QUERY_PER_GROUP)[:, None]
            allowed = (block_ids[None, :] >= lower_here) & (block_ids[None, :] < upper_here)
            masked = jnp.where(allowed, scores, -1e+30)
            row_max = lax.optimization_barrier(jnp.max(masked, axis=1, keepdims=True))
            exp_weights = jnp.where(allowed, jnp.exp(masked - row_max), 0.0)
            denominator = lax.optimization_barrier(jnp.sum(exp_weights, axis=1, keepdims=True))
            numerator = jnp.dot(exp_weights.astype(jnp.bfloat16), head_values, preferred_element_type=jnp.float32)
            return (numerator / denominator).astype(jnp.bfloat16).reshape(text_block, QUERY_PER_GROUP * HEAD_WIDTH)
        return lax.map(one_block, (head_queries, lower_rows, upper_rows)).reshape(TEXT_TOKENS, QUERY_PER_GROUP * HEAD_WIDTH)
    per_head_output = lax.map(single_head, jnp.arange(KEY_VALUE_HEADS).astype(jnp.int32))
    attended = jnp.transpose(per_head_output, (1, 0, 2)).reshape(TEXT_TOKENS, QUERY_HEADS * HEAD_WIDTH)
    summed = jnp.dot(attended, output_weight.reshape(QUERY_HEADS * HEAD_WIDTH, OUTPUT_FEATURES), preferred_element_type=jnp.float32)
    return (jnp.tanh(attn_gate[0]) * summed).astype(jnp.bfloat16)
```

```python
import functools
import math

import jax
import jax.numpy as jnp
from jax import lax
from jax.experimental import pallas as pl
from jax.experimental.pallas import tpu as pltpu
from jax.sharding import PartitionSpec as P

HEAD_WIDTH = 128
V_DEV = 128
INNER = 4
MESH = pl.DeviceIdType.MESH
very_low = -1e30


def kernel(
    frames,
    groups,
    q_ref,
    k_ref,
    v_ref,
    gain_ref,
    bounds_ref,
    w_ref,
    gate_ref,
    out_ref,
    kv,
    att,
    wbuf,
    obuf,
    kv_recv,
    kv_send,
    w_recv,
    w_send,
    wz_recv,
    wz_send,
    att_recv,
    att_send,
    out_recv,
    out_send,
    own_sem,
):
    depth = frames // INNER
    cols = wbuf.shape[4]
    tokens = q_ref.shape[0]
    heads = q_ref.shape[1] // HEAD_WIDTH
    f = lax.axis_index("frame")
    g = lax.axis_index("group")
    z = f // INNER
    a = f % INNER
    xb = a // 2
    cb = a % 2
    a_x = (1 - xb) * 2 + cb
    a_c = xb * 2 + (1 - cb)
    a_xc = (1 - xb) * 2 + (1 - cb)

    barrier = pltpu.get_barrier_semaphore()
    greeted = 0
    for step in range(1, frames):
        pl.semaphore_signal(
            barrier, inc=1, device_id=((f + step) % frames, g), device_id_type=MESH
        )
        greeted += 1
    for dg in range(1, groups):
        for da in range(INNER):
            pl.semaphore_signal(
                barrier,
                inc=1,
                device_id=(z * INNER + (a + da) % INNER, (g + dg) % groups),
                device_id_type=MESH,
            )
            greeted += 1
    kv[z, a, 0] = k_ref[...]
    kv[z, a, 1] = v_ref[...]
    pl.semaphore_wait(barrier, greeted)

    pending = []

    def send(src, dst, send_sem, recv_sem, to):
        copy = pltpu.make_async_remote_copy(
            src_ref=src,
            dst_ref=dst,
            send_sem=send_sem,
            recv_sem=recv_sem,
            device_id=to,
            device_id_type=MESH,
        )
        copy.start()
        pending.append(copy)

    def arrived(slot, send_sem, recv_sem):
        pltpu.make_async_remote_copy(
            src_ref=slot,
            dst_ref=slot,
            send_sem=send_sem,
            recv_sem=recv_sem,
            device_id=(z * INNER + a_x, g),
            device_id_type=MESH,
        ).wait_recv()

    n_kv = 0
    for dz in range(1, depth):
        send(
            kv.at[z, a],
            kv.at[z, a],
            kv_send.at[n_kv],
            kv_recv.at[z, a],
            ((z + dz) % depth * INNER + a, g),
        )
        n_kv += 1

    def columns(ga, aa):
        return pl.ds(pl.multiple_of((ga * INNER + aa) * cols, 128), cols)

    own = pltpu.make_async_copy(w_ref.at[0, :, columns(g, a)], wbuf.at[z, g, a], own_sem)
    own.start()
    n_w = 0
    for dg in range(groups):
        for da in range(INNER):
            if dg == 0 and da == 0:
                continue
            gg = (g + dg) % groups
            aa = (a + da) % INNER
            send(
                w_ref.at[0, :, columns(gg, aa)],
                wbuf.at[z, g, a],
                w_send.at[n_w],
                w_recv.at[g, a],
                (z * INNER + aa, gg),
            )
            n_w += 1

    for dz in range(depth):
        zz = (z + dz) % depth
        if dz:
            arrived(kv.at[zz, a], kv_send.at[0], kv_recv.at[zz, a])
        for aa in (a_x, a_c):
            send(
                kv.at[zz, a],
                kv.at[zz, a],
                kv_send.at[n_kv],
                kv_recv.at[zz, a],
                (z * INNER + aa, g),
            )
            n_kv += 1

    own.wait()
    n_wz = 0
    for dg in range(groups):
        gg = (g + dg) % groups
        for da in range(INNER):
            if dg == 0 and da == 0:
                continue
            aa = (a + da) % INNER
            arrived(wbuf.at[z, gg, aa], w_send.at[0], w_recv.at[gg, aa])
        for dz in range(1, depth):
            send(
                wbuf.at[z, gg],
                wbuf.at[z, gg],
                wz_send.at[n_wz],
                wz_recv.at[z, gg],
                ((z + dz) % depth * INNER + a, g),
            )
            n_wz += 1

    for dz in range(depth):
        zz = (z + dz) % depth
        arrived(kv.at[zz, a_x], kv_send.at[0], kv_recv.at[zz, a_x])
        send(
            kv.at[zz, a_x],
            kv.at[zz, a_x],
            kv_send.at[n_kv],
            kv_recv.at[zz, a_x],
            (z * INNER + a_c, g),
        )
        n_kv += 1
    for dz in range(depth):
        zz = (z + dz) % depth
        for aa in (a_c, a_xc):
            arrived(kv.at[zz, aa], kv_send.at[0], kv_recv.at[zz, aa])

    def spread(row):
        wide = jnp.broadcast_to(bounds_ref[row : row + 1, :].astype(jnp.float32), (tokens, tokens))
        return wide.T[:, :1].astype(jnp.int32)

    low = spread(0)
    high = spread(1)
    scale = 1.0 / math.sqrt(HEAD_WIDTH)
    chunk = INNER * V_DEV

    def one_head(h, carry):
        lanes = pl.ds(pl.multiple_of(h * HEAD_WIDTH, HEAD_WIDTH), HEAD_WIDTH)
        x = q_ref[:, lanes].astype(jnp.float32)
        x = x * lax.rsqrt(jnp.mean(x * x, axis=-1, keepdims=True) + 1e-05) * gain_ref[...]
        x = x.astype(jnp.bfloat16)
        top = jnp.full((tokens, 1), very_low, jnp.float32)
        total = jnp.zeros((tokens, 1), jnp.float32)
        summed = jnp.zeros((tokens, HEAD_WIDTH), jnp.float32)
        for zz in range(depth):
            keys = kv[zz, :, 0].reshape(chunk, HEAD_WIDTH)
            vals = kv[zz, :, 1].reshape(chunk, HEAD_WIDTH)
            scores = (
                lax.dot_general(
                    x, keys, (((1,), (1,)), ((), ())), preferred_element_type=jnp.float32
                )
                * scale
            )
            ids = zz * INNER + lax.broadcasted_iota(jnp.int32, (tokens, chunk), 1) // V_DEV
            allowed = (ids >= low) & (ids < high)
            masked = jnp.where(allowed, scores, very_low)
            newest = jnp.maximum(top, jnp.max(masked, axis=1, keepdims=True))
            weights = jnp.where(allowed, jnp.exp(masked - newest), 0.0)
            factor = jnp.exp(top - newest)
            total = total * factor + jnp.sum(weights, axis=1, keepdims=True)
            summed = summed * factor + jnp.dot(
                weights.astype(jnp.bfloat16), vals, preferred_element_type=jnp.float32
            )
            top = newest
        att[a, g, :, lanes] = (summed / total).astype(jnp.bfloat16)
        return carry

    lax.fori_loop(0, heads, one_head, 0)

    n_att = 0
    for dg in range(1, groups):
        send(
            att.at[a, g],
            att.at[a, g],
            att_send.at[n_att],
            att_recv.at[a, g],
            (f, (g + dg) % groups),
        )
        n_att += 1
    for dg in range(groups):
        gg = (g + dg) % groups
        if dg:
            arrived(att.at[a, gg], att_send.at[0], att_recv.at[a, gg])
        for aa in (a_x, a_c):
            send(
                att.at[a, gg],
                att.at[a, gg],
                att_send.at[n_att],
                att_recv.at[a, gg],
                (z * INNER + aa, g),
            )
            n_att += 1
    for dg in range(groups):
        gg = (g + dg) % groups
        arrived(att.at[a_x, gg], att_send.at[0], att_recv.at[a_x, gg])
        send(
            att.at[a_x, gg],
            att.at[a_x, gg],
            att_send.at[n_att],
            att_recv.at[a_x, gg],
            (z * INNER + a_c, g),
        )
        n_att += 1
    for dg in range(groups):
        gg = (g + dg) % groups
        for aa in (a_c, a_xc):
            arrived(att.at[aa, gg], att_send.at[0], att_recv.at[aa, gg])
    for dz in range(1, depth):
        zz = (z + dz) % depth
        for dg in range(groups):
            gg = (g + dg) % groups
            arrived(wbuf.at[zz, gg], wz_send.at[0], wz_recv.at[zz, gg])

    gate = jnp.tanh(gate_ref[...])
    width = heads * HEAD_WIDTH
    for j in range(INNER):
        aa = (a + 1 + j) % INNER
        acc = jnp.zeros((tokens, cols), jnp.float32)
        for gg in range(groups):
            acc = acc + jnp.dot(
                att[aa, gg], wbuf[:, gg].reshape(width, cols), preferred_element_type=jnp.float32
            )
        done = (gate * acc).astype(jnp.bfloat16)
        mine = pl.ds(pl.multiple_of(a * cols, 128), cols)
        if j == INNER - 1:
            out_ref[:, mine] = done
        else:
            obuf[j] = done
            send(
                obuf.at[j],
                out_ref.at[:, mine],
                out_send.at[j],
                out_recv.at[a],
                (z * INNER + aa, g),
            )
    for da in range(1, INNER):
        aa = (a + da) % INNER
        there = pl.ds(pl.multiple_of(aa * cols, 128), cols)
        arrived(out_ref.at[:, there], out_send.at[0], out_recv.at[aa])
    for copy in pending:
        copy.wait_send()


def local(queries, keys, values, q_gain, frame_bounds, output_weight, attn_gate):
    frames = lax.axis_size("frame")
    groups = lax.axis_size("group")
    tokens, width = queries.shape
    rows = output_weight.shape[1]
    cols = output_weight.shape[2] // (groups * INNER)
    depth = frames // INNER
    dma = pltpu.SemaphoreType.DMA
    vmem = pl.BlockSpec(memory_space=pltpu.VMEM)
    plane = groups * INNER
    return pl.pallas_call(
        functools.partial(kernel, frames, groups),
        out_shape=jax.ShapeDtypeStruct((tokens, INNER * cols), jnp.bfloat16),
        in_specs=[vmem] * 7,
        out_specs=vmem,
        scratch_shapes=[
            pltpu.VMEM((depth, INNER, 2, keys.shape[0], HEAD_WIDTH), jnp.bfloat16),
            pltpu.VMEM((INNER, groups, tokens, width), jnp.bfloat16),
            pltpu.VMEM((depth, groups, INNER, rows, cols), jnp.bfloat16),
            pltpu.VMEM((INNER - 1, tokens, cols), jnp.bfloat16),
            dma((depth, INNER)),
            dma((4 * depth - 1,)),
            dma((groups, INNER)),
            dma((plane - 1,)),
            dma((depth, groups)),
            dma((groups * (depth - 1),)),
            dma((INNER, groups)),
            dma((4 * groups - 1,)),
            dma((INNER,)),
            dma((INNER - 1,)),
            dma(()),
        ],
        compiler_params=pltpu.CompilerParams(
            collective_id=0, has_side_effects=True, vmem_limit_bytes=48 * 1024 * 1024
        ),
        cost_estimate=pl.CostEstimate(
            flops=3 * 1024**3, bytes_accessed=4 * 1024**2, transcendentals=2 * 1024**2
        ),
    )(
        queries,
        keys,
        values,
        q_gain.reshape(1, HEAD_WIDTH),
        frame_bounds,
        output_weight,
        attn_gate.reshape(1, 1),
    )


def solution(mesh):
    placed = (
        P("frame", "group"),
        P("frame", "group"),
        P("frame", "group"),
        P(),
        P(None, "frame"),
        P("group", "frame", None),
        P(),
    )
    return jax.shard_map(
        local, mesh=mesh, in_specs=placed, out_specs=P("frame", "group"), check_vma=False
    )
```

```python
import functools
import math

import jax
import jax.numpy as jnp
from jax import lax
from jax.experimental import pallas as pl
from jax.experimental.pallas import tpu as pltpu
from jax.sharding import PartitionSpec as P

HEAD_WIDTH = 128
V_DEV = 128
INNER = 4
MESH = pl.DeviceIdType.MESH
very_low = -1e30


def kernel(
    frames,
    groups,
    q_hbm,
    k_hbm,
    v_hbm,
    gain_hbm,
    bounds_hbm,
    w_ref,
    gate_ref,
    out_ref,
    q_ref,
    gain_ref,
    bounds_ref,
    kv,
    att,
    wbuf,
    obuf,
    kv_recv,
    kv_send,
    w_recv,
    w_send,
    wz_recv,
    wz_send,
    att_recv,
    att_send,
    out_recv,
    out_send,
    own_sem,
    in_sem,
):
    depth = frames // INNER
    halves = wbuf.shape[0]
    half = wbuf.shape[5]
    cols = halves * half
    tokens = q_ref.shape[0]
    heads = q_ref.shape[1] // HEAD_WIDTH
    f = lax.axis_index("frame")
    g = lax.axis_index("group")
    z = f // INNER
    a = f % INNER
    xb = a // 2
    cb = a % 2
    a_x = (1 - xb) * 2 + cb
    a_c = xb * 2 + (1 - cb)
    a_xc = (1 - xb) * 2 + (1 - cb)

    barrier = pltpu.get_barrier_semaphore()
    greeted = 0
    others = [((z + dz) % depth * INNER + a, g) for dz in range(1, depth)]
    others += [(z * INNER + (a + da) % INNER, g) for da in range(1, INNER)]
    for other in others:
        pl.semaphore_signal(barrier, inc=1, device_id=other, device_id_type=MESH)
        greeted += 1
    for dg in range(1, groups):
        for da in range(INNER):
            pl.semaphore_signal(
                barrier,
                inc=1,
                device_id=(z * INNER + (a + da) % INNER, (g + dg) % groups),
                device_id_type=MESH,
            )
            greeted += 1
    brought = [
        pltpu.make_async_copy(source, target, in_sem.at[i])
        for i, (source, target) in enumerate(
            (
                (k_hbm, kv.at[z, a, 0]),
                (v_hbm, kv.at[z, a, 1]),
                (q_hbm, q_ref),
                (gain_hbm, gain_ref),
                (bounds_hbm, bounds_ref),
            )
        )
    ]
    for copy in brought:
        copy.start()
    brought[0].wait()
    brought[1].wait()
    pl.semaphore_wait(barrier, greeted)

    pending = []
    pending_if = []

    def send(src, dst, send_sem, recv_sem, to):
        copy = pltpu.make_async_remote_copy(
            src_ref=src,
            dst_ref=dst,
            send_sem=send_sem,
            recv_sem=recv_sem,
            device_id=to,
            device_id_type=MESH,
        )
        copy.start()
        pending.append(copy)

    def arrived(slot, send_sem, recv_sem):
        pltpu.make_async_remote_copy(
            src_ref=slot,
            dst_ref=slot,
            send_sem=send_sem,
            recv_sem=recv_sem,
            device_id=(z * INNER + a_x, g),
            device_id_type=MESH,
        ).wait_recv()

    n_kv = 0
    for dz in range(1, depth):
        send(
            kv.at[z, a],
            kv.at[z, a],
            kv_send.at[n_kv],
            kv_recv.at[z, a],
            ((z + dz) % depth * INNER + a, g),
        )
        n_kv += 1

    def columns(ga, aa, part):
        start = (ga * INNER + aa) * cols + part * half
        return pl.ds(pl.multiple_of(start, half), half)

    own = [
        pltpu.make_async_copy(
            w_ref.at[0, :, columns(g, a, part)], wbuf.at[part, z, g, a], own_sem.at[part]
        )
        for part in range(halves)
    ]
    n_w = 0
    for part in range(halves):
        own[part].start()
        for dg in range(groups):
            for da in range(INNER):
                if dg == 0 and da == 0:
                    continue
                gg = (g + dg) % groups
                aa = (a + da) % INNER
                send(
                    w_ref.at[0, :, columns(gg, aa, part)],
                    wbuf.at[part, z, g, a],
                    w_send.at[n_w],
                    w_recv.at[part, g, a],
                    (z * INNER + aa, gg),
                )
                n_w += 1

    for dz in range(depth):
        zz = (z + dz) % depth
        if dz:
            arrived(kv.at[zz, a], kv_send.at[0], kv_recv.at[zz, a])
        for aa in (a_x, a_c):
            send(
                kv.at[zz, a],
                kv.at[zz, a],
                kv_send.at[n_kv],
                kv_recv.at[zz, a],
                (z * INNER + aa, g),
            )
            n_kv += 1

    def pass_on(block, part, to, exists, way, hop):
        copy = pltpu.make_async_remote_copy(
            src_ref=wbuf.at[part, block],
            dst_ref=wbuf.at[part, block],
            send_sem=wz_send.at[way, hop, part],
            recv_sem=wz_recv.at[block, part],
            device_id=(to * INNER + a, g),
            device_id_type=MESH,
        )
        pending_if.append((exists, copy))
        return copy

    def below_above(hop, part):
        below = z - hop
        above = z + hop
        for block, to, way in ((below, z + 1, 0), (above, z - 1, 1)):
            here = block >= 0 if way == 0 else block < depth
            onward = to < depth if way == 0 else to >= 0
            at = lax.clamp(0, block, depth - 1)
            exists = jnp.logical_and(here, onward)
            if hop:

                @pl.when(here)
                def _():
                    arrived(wbuf.at[part, at], wz_send.at[0, 0, 0], wz_recv.at[at, part])

            if hop < depth - 1:
                copy = pass_on(at, part, lax.clamp(0, to, depth - 1), exists, way, hop)

                @pl.when(exists)
                def _():
                    copy.start()

    for part in range(halves):
        own[part].wait()
        for dg in range(groups):
            gg = (g + dg) % groups
            for da in range(INNER):
                if dg == 0 and da == 0:
                    continue
                aa = (a + da) % INNER
                arrived(wbuf.at[part, z, gg, aa], w_send.at[0], w_recv.at[part, gg, aa])
        below_above(0, part)

    for dz in range(depth):
        zz = (z + dz) % depth
        arrived(kv.at[zz, a_x], kv_send.at[0], kv_recv.at[zz, a_x])
        send(
            kv.at[zz, a_x],
            kv.at[zz, a_x],
            kv_send.at[n_kv],
            kv_recv.at[zz, a_x],
            (z * INNER + a_c, g),
        )
        n_kv += 1
    for dz in range(depth):
        zz = (z + dz) % depth
        for aa in (a_c, a_xc):
            arrived(kv.at[zz, aa], kv_send.at[0], kv_recv.at[zz, aa])

    for copy in brought[2:]:
        copy.wait()

    def spread(row):
        wide = jnp.broadcast_to(bounds_ref[row : row + 1, :].astype(jnp.float32), (tokens, tokens))
        return wide.T[:, :1].astype(jnp.int32)

    low = spread(0)
    high = spread(1)
    scale = 1.0 / math.sqrt(HEAD_WIDTH)
    chunk = INNER * V_DEV

    def one_head(h, carry):
        lanes = pl.ds(pl.multiple_of(h * HEAD_WIDTH, HEAD_WIDTH), HEAD_WIDTH)
        x = q_ref[:, lanes].astype(jnp.float32)
        x = x * lax.rsqrt(jnp.mean(x * x, axis=-1, keepdims=True) + 1e-05) * gain_ref[...]
        x = x.astype(jnp.bfloat16)
        top = jnp.full((tokens, 1), very_low, jnp.float32)
        total = jnp.zeros((tokens, 1), jnp.float32)
        summed = jnp.zeros((tokens, HEAD_WIDTH), jnp.float32)
        for zz in range(depth):
            keys = kv[zz, :, 0].reshape(chunk, HEAD_WIDTH)
            vals = kv[zz, :, 1].reshape(chunk, HEAD_WIDTH)
            scores = (
                lax.dot_general(
                    x, keys, (((1,), (1,)), ((), ())), preferred_element_type=jnp.float32
                )
                * scale
            )
            ids = zz * INNER + lax.broadcasted_iota(jnp.int32, (tokens, chunk), 1) // V_DEV
            allowed = (ids >= low) & (ids < high)
            masked = jnp.where(allowed, scores, very_low)
            newest = jnp.maximum(top, jnp.max(masked, axis=1, keepdims=True))
            weights = jnp.where(allowed, jnp.exp(masked - newest), 0.0)
            factor = jnp.exp(top - newest)
            total = total * factor + jnp.sum(weights, axis=1, keepdims=True)
            summed = summed * factor + jnp.dot(
                weights.astype(jnp.bfloat16), vals, preferred_element_type=jnp.float32
            )
            top = newest
        att[a, g, :, lanes] = (summed / total).astype(jnp.bfloat16)
        return carry

    lax.fori_loop(0, heads // 2, one_head, 0)
    below_above(1, 0)
    lax.fori_loop(heads // 2, heads, one_head, 0)

    n_att = 0
    for dg in range(1, groups):
        send(
            att.at[a, g],
            att.at[a, g],
            att_send.at[n_att],
            att_recv.at[a, g],
            (f, (g + dg) % groups),
        )
        n_att += 1
    for hop in range(2, depth - 1):
        below_above(hop, 0)
    for dg in range(groups):
        gg = (g + dg) % groups
        if dg:
            arrived(att.at[a, gg], att_send.at[0], att_recv.at[a, gg])
        for aa in (a_x, a_c):
            send(
                att.at[a, gg],
                att.at[a, gg],
                att_send.at[n_att],
                att_recv.at[a, gg],
                (z * INNER + aa, g),
            )
            n_att += 1
    for part in range(1, halves):
        for hop in range(1, depth - 1):
            below_above(hop, part)
    for dg in range(groups):
        gg = (g + dg) % groups
        arrived(att.at[a_x, gg], att_send.at[0], att_recv.at[a_x, gg])
        send(
            att.at[a_x, gg],
            att.at[a_x, gg],
            att_send.at[n_att],
            att_recv.at[a_x, gg],
            (z * INNER + a_c, g),
        )
        n_att += 1
    for dg in range(groups):
        gg = (g + dg) % groups
        for aa in (a_c, a_xc):
            arrived(att.at[aa, gg], att_send.at[0], att_recv.at[aa, gg])

    gate = jnp.tanh(gate_ref[...])
    width = heads * HEAD_WIDTH

    def target(aa, part):
        return pl.ds(pl.multiple_of(aa * cols + part * half, half), half)

    for part in range(halves):
        below_above(depth - 1, part)
        acc = jnp.zeros((INNER * tokens, half), jnp.float32)
        for gg in range(groups):
            acc = acc + jnp.dot(
                att[:, gg].reshape(INNER * tokens, width),
                wbuf[part, :, gg].reshape(width, half),
                preferred_element_type=jnp.float32,
            )
        done = (gate * acc).astype(jnp.bfloat16)
        obuf[part] = done.reshape(INNER, tokens, half)
        for da in (2, 3, 1):
            aa = (a + da) % INNER
            send(
                obuf.at[part, aa],
                out_ref.at[:, target(a, part)],
                out_send.at[part, da - 1],
                out_recv.at[part, a],
                (z * INNER + aa, g),
            )
        out_ref[:, target(a, part)] = obuf[part, a]
    for part in range(halves):
        for da in range(1, INNER):
            aa = (a + da) % INNER
            arrived(out_ref.at[:, target(aa, part)], out_send.at[0, 0], out_recv.at[part, aa])
    for copy in pending:
        copy.wait_send()
    for exists, copy in pending_if:

        @pl.when(exists)
        def _():
            copy.wait_send()


def local(queries, keys, values, q_gain, frame_bounds, output_weight, attn_gate):
    frames = lax.axis_size("frame")
    groups = lax.axis_size("group")
    tokens, width = queries.shape
    rows = output_weight.shape[1]
    cols = output_weight.shape[2] // (groups * INNER)
    depth = frames // INNER
    dma = pltpu.SemaphoreType.DMA
    vmem = pl.BlockSpec(memory_space=pltpu.VMEM)
    plane = groups * INNER
    halves = 2 if cols % 256 == 0 else 1
    half = cols // halves
    anywhere = pl.BlockSpec(memory_space=pl.ANY)
    return pl.pallas_call(
        functools.partial(kernel, frames, groups),
        out_shape=jax.ShapeDtypeStruct((tokens, INNER * cols), jnp.bfloat16),
        in_specs=[anywhere] * 6 + [vmem],
        out_specs=vmem,
        scratch_shapes=[
            pltpu.VMEM((tokens, width), jnp.bfloat16),
            pltpu.VMEM((1, HEAD_WIDTH), jnp.float32),
            pltpu.VMEM((2, tokens), jnp.int32),
            pltpu.VMEM((depth, INNER, 2, keys.shape[0], HEAD_WIDTH), jnp.bfloat16),
            pltpu.VMEM((INNER, groups, tokens, width), jnp.bfloat16),
            pltpu.VMEM((halves, depth, groups, INNER, rows, half), jnp.bfloat16),
            pltpu.VMEM((halves, INNER, tokens, half), jnp.bfloat16),
            dma((depth, INNER)),
            dma((4 * depth - 1,)),
            dma((halves, groups, INNER)),
            dma((halves * (plane - 1),)),
            dma((depth, halves)),
            dma((2, depth - 1, halves)),
            dma((INNER, groups)),
            dma((4 * groups - 1,)),
            dma((halves, INNER)),
            dma((halves, INNER - 1)),
            dma((halves,)),
            dma((5,)),
        ],
        compiler_params=pltpu.CompilerParams(
            collective_id=0, has_side_effects=True, vmem_limit_bytes=60 * 1024 * 1024
        ),
        cost_estimate=pl.CostEstimate(
            flops=3 * 1024**3, bytes_accessed=4 * 1024**2, transcendentals=2 * 1024**2
        ),
    )(
        queries,
        keys,
        values,
        q_gain.reshape(1, HEAD_WIDTH),
        frame_bounds,
        output_weight,
        attn_gate.reshape(1, 1),
    )


def solution(mesh):
    placed = (
        P("frame", "group"),
        P("frame", "group"),
        P("frame", "group"),
        P(),
        P(None, "frame"),
        P("group", "frame", None),
        P(),
    )
    return jax.shard_map(
        local, mesh=mesh, in_specs=placed, out_specs=P("frame", "group"), check_vma=False
    )
```

```python
import functools
import math

import jax
import jax.numpy as jnp
from jax import lax
from jax.experimental import pallas as pl
from jax.experimental.pallas import tpu as pltpu
from jax.sharding import PartitionSpec as P

HEAD_WIDTH = 128
V_DEV = 128
INNER = 4
MESH = pl.DeviceIdType.MESH
very_low = -1e30


def kernel(
    frames,
    groups,
    q_hbm,
    k_hbm,
    v_hbm,
    gain_hbm,
    bounds_hbm,
    w_ref,
    gate_ref,
    out_ref,
    q_ref,
    gain_ref,
    bounds_ref,
    bias,
    logits,
    kv,
    att,
    wbuf,
    obuf,
    kv_recv,
    kv_send,
    w_recv,
    w_send,
    wz_recv,
    wz_send,
    att_recv,
    att_send,
    out_recv,
    out_send,
    own_sem,
    in_sem,
):
    depth = frames // INNER
    halves = wbuf.shape[0]
    half = wbuf.shape[5]
    cols = halves * half
    parts = att.shape[0]
    tokens = q_ref.shape[0]
    heads = q_ref.shape[1] // HEAD_WIDTH
    f = lax.axis_index("frame")
    g = lax.axis_index("group")
    z = f // INNER
    a = f % INNER
    xb = a // 2
    cb = a % 2
    a_x = (1 - xb) * 2 + cb
    a_c = xb * 2 + (1 - cb)
    a_xc = (1 - xb) * 2 + (1 - cb)

    barrier = pltpu.get_barrier_semaphore()
    greeted = 0
    others = [((z + dz) % depth * INNER + a, g) for dz in range(1, depth)]
    others += [(z * INNER + (a + da) % INNER, g) for da in range(1, INNER)]
    for other in others:
        pl.semaphore_signal(barrier, inc=1, device_id=other, device_id_type=MESH)
        greeted += 1
    for dg in range(1, groups):
        for da in range(INNER):
            pl.semaphore_signal(
                barrier,
                inc=1,
                device_id=(z * INNER + (a + da) % INNER, (g + dg) % groups),
                device_id_type=MESH,
            )
            greeted += 1
    brought = [
        pltpu.make_async_copy(source, target, in_sem.at[i])
        for i, (source, target) in enumerate(
            (
                (k_hbm, kv.at[z, a, 0]),
                (v_hbm, kv.at[z, a, 1]),
                (q_hbm, q_ref),
                (gain_hbm, gain_ref),
                (bounds_hbm, bounds_ref),
            )
        )
    ]
    for copy in brought:
        copy.start()
    brought[0].wait()
    brought[1].wait()
    pl.semaphore_wait(barrier, greeted)

    pending = []
    pending_if = []

    def send(src, dst, send_sem, recv_sem, to):
        copy = pltpu.make_async_remote_copy(
            src_ref=src,
            dst_ref=dst,
            send_sem=send_sem,
            recv_sem=recv_sem,
            device_id=to,
            device_id_type=MESH,
        )
        copy.start()
        pending.append(copy)

    def arrived(slot, send_sem, recv_sem):
        pltpu.make_async_remote_copy(
            src_ref=slot,
            dst_ref=slot,
            send_sem=send_sem,
            recv_sem=recv_sem,
            device_id=(z * INNER + a_x, g),
            device_id_type=MESH,
        ).wait_recv()

    n_kv = 0
    for dz in range(1, depth):
        send(
            kv.at[z, a],
            kv.at[z, a],
            kv_send.at[n_kv],
            kv_recv.at[z, a],
            ((z + dz) % depth * INNER + a, g),
        )
        n_kv += 1

    def columns(ga, aa, part):
        start = (ga * INNER + aa) * cols + part * half
        return pl.ds(pl.multiple_of(start, half), half)

    own = [
        pltpu.make_async_copy(
            w_ref.at[0, :, columns(g, a, part)], wbuf.at[part, z, g, a], own_sem.at[part]
        )
        for part in range(halves)
    ]
    n_w = 0
    for part in range(halves):
        own[part].start()
        for dg in range(groups):
            for da in range(INNER):
                if dg == 0 and da == 0:
                    continue
                gg = (g + dg) % groups
                aa = (a + da) % INNER
                send(
                    w_ref.at[0, :, columns(gg, aa, part)],
                    wbuf.at[part, z, g, a],
                    w_send.at[n_w],
                    w_recv.at[part, g, a],
                    (z * INNER + aa, gg),
                )
                n_w += 1

    for copy in brought[2:]:
        copy.wait()

    def spread(row):
        wide = jnp.broadcast_to(
            bounds_ref[row : row + 1, :].astype(jnp.float32), (V_DEV, tokens)
        )
        return wide.T

    low = spread(0)
    high = spread(1)
    for block in range(frames):
        allowed = (low <= block) & (high > block)
        bias[:, block * V_DEV : (block + 1) * V_DEV] = jnp.where(allowed, 0.0, very_low)

    def pass_on(block, part, to, exists, way, hop):
        copy = pltpu.make_async_remote_copy(
            src_ref=wbuf.at[part, block],
            dst_ref=wbuf.at[part, block],
            send_sem=wz_send.at[way, hop, part],
            recv_sem=wz_recv.at[block, part],
            device_id=(to * INNER + a, g),
            device_id_type=MESH,
        )
        pending_if.append((exists, copy))
        return copy

    def below_above(hop, part):
        below = z - hop
        above = z + hop
        for block, to, way in ((below, z + 1, 0), (above, z - 1, 1)):
            here = block >= 0 if way == 0 else block < depth
            onward = to < depth if way == 0 else to >= 0
            at = lax.clamp(0, block, depth - 1)
            exists = jnp.logical_and(here, onward)
            if hop:

                @pl.when(here)
                def _():
                    arrived(wbuf.at[part, at], wz_send.at[0, 0, 0], wz_recv.at[at, part])

            if hop < depth - 1:
                copy = pass_on(at, part, lax.clamp(0, to, depth - 1), exists, way, hop)

                @pl.when(exists)
                def _():
                    copy.start()

    def begin(part):
        own[part].wait()
        for dg in range(groups):
            gg = (g + dg) % groups
            for da in range(INNER):
                if dg == 0 and da == 0:
                    continue
                aa = (a + da) % INNER
                arrived(wbuf.at[part, z, gg, aa], w_send.at[0], w_recv.at[part, gg, aa])
        below_above(0, part)

    begin(0)

    for dz in range(depth):
        zz = (z + dz) % depth
        if dz:
            arrived(kv.at[zz, a], kv_send.at[0], kv_recv.at[zz, a])
        for aa in (a_x, a_c):
            send(
                kv.at[zz, a],
                kv.at[zz, a],
                kv_send.at[n_kv],
                kv_recv.at[zz, a],
                (z * INNER + aa, g),
            )
            n_kv += 1

    for part in range(1, halves):
        begin(part)

    for dz in range(depth):
        zz = (z + dz) % depth
        arrived(kv.at[zz, a_x], kv_send.at[0], kv_recv.at[zz, a_x])
        send(
            kv.at[zz, a_x],
            kv.at[zz, a_x],
            kv_send.at[n_kv],
            kv_recv.at[zz, a_x],
            (z * INNER + a_c, g),
        )
        n_kv += 1
    for dz in range(depth):
        zz = (z + dz) % depth
        for aa in (a_c, a_xc):
            arrived(kv.at[zz, aa], kv_send.at[0], kv_recv.at[zz, aa])

    fold = math.log2(math.e) / math.sqrt(HEAD_WIDTH)
    per = heads // parts
    rows = per * tokens
    pair = 2 * V_DEV

    def attend(part):
        normed = []
        for h in range(part * per, (part + 1) * per):
            x = q_ref[:, h * HEAD_WIDTH : (h + 1) * HEAD_WIDTH].astype(jnp.float32)
            x = x * lax.rsqrt(jnp.mean(x * x, axis=-1, keepdims=True) + 1e-05) * gain_ref[...]
            normed.append(x.astype(jnp.bfloat16))
        x = jnp.concatenate(normed, axis=0)
        top = jnp.full((rows, V_DEV), very_low, jnp.float32)
        for n in range(frames // 2):
            at = n * 2 // INNER
            first = n * 2 % INNER
            keys = kv[at, first : first + 2, 0].reshape(pair, HEAD_WIDTH)
            scores = lax.dot_general(
                x, keys, (((1,), (1,)), ((), ())), preferred_element_type=jnp.float32
            )
            offset = bias[:, n * pair : (n + 1) * pair]
            scores = scores * fold + jnp.concatenate([offset] * per, axis=0)
            logits[:, n * pair : (n + 1) * pair] = scores
            top = jnp.maximum(top, jnp.maximum(scores[:, :V_DEV], scores[:, V_DEV:]))
        top = jnp.max(top, axis=1, keepdims=True)
        total = jnp.zeros((rows, V_DEV), jnp.float32)
        summed = jnp.zeros((rows, HEAD_WIDTH), jnp.float32)
        for n in range(frames // 2):
            at = n * 2 // INNER
            first = n * 2 % INNER
            vals = kv[at, first : first + 2, 1].reshape(pair, HEAD_WIDTH)
            weights = jnp.exp2(logits[:, n * pair : (n + 1) * pair] - top)
            total = total + (weights[:, :V_DEV] + weights[:, V_DEV:])
            summed = summed + jnp.dot(
                weights.astype(jnp.bfloat16), vals, preferred_element_type=jnp.float32
            )
        total = jnp.sum(total, axis=1, keepdims=True)
        result = (summed / total).astype(jnp.bfloat16)
        for h in range(per):
            att[part, a, g, :, h * HEAD_WIDTH : (h + 1) * HEAD_WIDTH] = result[
                h * tokens : (h + 1) * tokens
            ]

    n_att = [0]

    def hand(part, aa, gg, to):
        send(
            att.at[part, aa, gg],
            att.at[part, aa, gg],
            att_send.at[n_att[0]],
            att_recv.at[part, aa, gg],
            to,
        )
        n_att[0] += 1

    def await_att(part, aa, gg):
        arrived(att.at[part, aa, gg], att_send.at[0], att_recv.at[part, aa, gg])

    tasks = [(hop, part) for hop in range(1, depth - 1) for part in range(halves)]
    steps = parts + 2
    for step in range(steps):
        if step < parts:
            attend(step)
        for hop, part in tasks[-(-step * len(tasks) // steps) : -(-(step + 1) * len(tasks) // steps)]:
            below_above(hop, part)
        if step < parts:
            for dg in range(1, groups):
                hand(step, a, g, (f, (g + dg) % groups))
            for aa in (a_x, a_c):
                hand(step, a, g, (z * INNER + aa, g))
        if 1 <= step <= parts:
            for dg in range(1, groups):
                gg = (g + dg) % groups
                await_att(step - 1, a, gg)
                for aa in (a_x, a_c):
                    hand(step - 1, a, gg, (z * INNER + aa, g))
        if step >= 2:
            for dg in range(groups):
                gg = (g + dg) % groups
                await_att(step - 2, a_x, gg)
                hand(step - 2, a_x, gg, (z * INNER + a_c, g))
    for part in range(parts):
        for dg in range(groups):
            gg = (g + dg) % groups
            for aa in (a_c, a_xc):
                await_att(part, aa, gg)

    gate = jnp.tanh(gate_ref[...])
    width = heads * HEAD_WIDTH

    def target(aa, part):
        return pl.ds(pl.multiple_of(aa * cols + part * half, half), half)

    for part in range(halves):
        below_above(depth - 1, part)
        acc = jnp.zeros((INNER * tokens, half), jnp.float32)
        for gg in range(groups):
            weight = wbuf[part, :, gg].reshape(width, half)
            for p in range(parts):
                acc = acc + jnp.dot(
                    att[p, :, gg].reshape(INNER * tokens, width // parts),
                    weight[p * (width // parts) : (p + 1) * (width // parts)],
                    preferred_element_type=jnp.float32,
                )
        done = (gate * acc).astype(jnp.bfloat16)
        obuf[part] = done.reshape(INNER, tokens, half)
        for da in (2, 3, 1):
            aa = (a + da) % INNER
            send(
                obuf.at[part, aa],
                out_ref.at[:, target(a, part)],
                out_send.at[part, da - 1],
                out_recv.at[part, a],
                (z * INNER + aa, g),
            )
        out_ref[:, target(a, part)] = obuf[part, a]
    for part in range(halves):
        for da in range(1, INNER):
            aa = (a + da) % INNER
            arrived(out_ref.at[:, target(aa, part)], out_send.at[0, 0], out_recv.at[part, aa])
    for copy in pending:
        copy.wait_send()
    for exists, copy in pending_if:

        @pl.when(exists)
        def _():
            copy.wait_send()


def local(queries, keys, values, q_gain, frame_bounds, output_weight, attn_gate):
    frames = lax.axis_size("frame")
    groups = lax.axis_size("group")
    tokens, width = queries.shape
    rows = output_weight.shape[1]
    cols = output_weight.shape[2] // (groups * INNER)
    depth = frames // INNER
    dma = pltpu.SemaphoreType.DMA
    vmem = pl.BlockSpec(memory_space=pltpu.VMEM)
    plane = groups * INNER
    heads = width // HEAD_WIDTH
    parts = 4
    per = heads // parts
    halves = cols // 128
    half = cols // halves
    anywhere = pl.BlockSpec(memory_space=pl.ANY)
    return pl.pallas_call(
        functools.partial(kernel, frames, groups),
        out_shape=jax.ShapeDtypeStruct((tokens, INNER * cols), jnp.bfloat16),
        in_specs=[anywhere] * 6 + [vmem],
        out_specs=vmem,
        scratch_shapes=[
            pltpu.VMEM((tokens, width), jnp.bfloat16),
            pltpu.VMEM((1, HEAD_WIDTH), jnp.float32),
            pltpu.VMEM((2, tokens), jnp.int32),
            pltpu.VMEM((tokens, frames * V_DEV), jnp.float32),
            pltpu.VMEM((per * tokens, frames * V_DEV), jnp.float32),
            pltpu.VMEM((depth, INNER, 2, keys.shape[0], HEAD_WIDTH), jnp.bfloat16),
            pltpu.VMEM((parts, INNER, groups, tokens, width // parts), jnp.bfloat16),
            pltpu.VMEM((halves, depth, groups, INNER, rows, half), jnp.bfloat16),
            pltpu.VMEM((halves, INNER, tokens, half), jnp.bfloat16),
            dma((depth, INNER)),
            dma((4 * depth - 1,)),
            dma((halves, groups, INNER)),
            dma((halves * (plane - 1),)),
            dma((depth, halves)),
            dma((2, depth - 1, halves)),
            dma((parts, INNER, groups)),
            dma((parts * (4 * groups - 1),)),
            dma((halves, INNER)),
            dma((halves, INNER - 1)),
            dma((halves,)),
            dma((5,)),
        ],
        compiler_params=pltpu.CompilerParams(
            collective_id=0, has_side_effects=True, vmem_limit_bytes=60 * 1024 * 1024
        ),
        cost_estimate=pl.CostEstimate(
            flops=3 * 1024**3, bytes_accessed=4 * 1024**2, transcendentals=2 * 1024**2
        ),
    )(
        queries,
        keys,
        values,
        q_gain.reshape(1, HEAD_WIDTH),
        frame_bounds,
        output_weight,
        attn_gate.reshape(1, 1),
    )


def solution(mesh):
    placed = (
        P("frame", "group"),
        P("frame", "group"),
        P("frame", "group"),
        P(),
        P(None, "frame"),
        P("group", "frame", None),
        P(),
    )
    return jax.shard_map(
        local, mesh=mesh, in_specs=placed, out_specs=P("frame", "group"), check_vma=False
    )
```

```python
import functools
import math

import jax
import jax.numpy as jnp
from jax import lax
from jax.experimental import pallas as pl
from jax.experimental.pallas import tpu as pltpu
from jax.sharding import PartitionSpec as P

HEAD_WIDTH = 128
V_DEV = 128
INNER = 4
MESH = pl.DeviceIdType.MESH
very_low = -1e30


def kernel(
    frames,
    groups,
    q_hbm,
    k_hbm,
    v_hbm,
    gain_hbm,
    bounds_hbm,
    w_ref,
    gate_ref,
    out_ref,
    q_ref,
    gain_ref,
    bounds_ref,
    bias,
    logits,
    kv,
    att,
    wbuf,
    obuf,
    kv_recv,
    kv_send,
    w_recv,
    w_send,
    wz_recv,
    wz_send,
    att_recv,
    att_send,
    out_recv,
    out_send,
    own_sem,
    in_sem,
):
    depth = frames // INNER
    halves = wbuf.shape[0]
    half = wbuf.shape[5]
    cols = halves * half
    parts = att.shape[0]
    tokens = q_ref.shape[0]
    heads = q_ref.shape[1] // HEAD_WIDTH
    f = lax.axis_index("frame")
    g = lax.axis_index("group")
    z = f // INNER
    a = f % INNER
    xb = a // 2
    cb = a % 2
    a_x = (1 - xb) * 2 + cb
    a_c = xb * 2 + (1 - cb)
    a_xc = (1 - xb) * 2 + (1 - cb)

    barrier = pltpu.get_barrier_semaphore()
    greeted = 0
    others = [((z + dz) % depth * INNER + a, g) for dz in range(1, depth)]
    others += [(z * INNER + (a + da) % INNER, g) for da in range(1, INNER)]
    for other in others:
        pl.semaphore_signal(barrier, inc=1, device_id=other, device_id_type=MESH)
        greeted += 1
    for dg in range(1, groups):
        for da in range(INNER):
            pl.semaphore_signal(
                barrier,
                inc=1,
                device_id=(z * INNER + (a + da) % INNER, (g + dg) % groups),
                device_id_type=MESH,
            )
            greeted += 1
    brought = [
        pltpu.make_async_copy(source, target, in_sem.at[i])
        for i, (source, target) in enumerate(
            (
                (k_hbm, kv.at[z, a, 0]),
                (v_hbm, kv.at[z, a, 1]),
                (q_hbm, q_ref),
                (gain_hbm, gain_ref),
                (bounds_hbm, bounds_ref),
            )
        )
    ]
    for copy in brought:
        copy.start()
    brought[0].wait()
    brought[1].wait()
    pl.semaphore_wait(barrier, greeted)

    pending = []
    pending_if = []

    def send(src, dst, send_sem, recv_sem, to):
        copy = pltpu.make_async_remote_copy(
            src_ref=src,
            dst_ref=dst,
            send_sem=send_sem,
            recv_sem=recv_sem,
            device_id=to,
            device_id_type=MESH,
        )
        copy.start()
        pending.append(copy)

    def arrived(slot, send_sem, recv_sem):
        pltpu.make_async_remote_copy(
            src_ref=slot,
            dst_ref=slot,
            send_sem=send_sem,
            recv_sem=recv_sem,
            device_id=(z * INNER + a_x, g),
            device_id_type=MESH,
        ).wait_recv()

    n_kv = 0
    for dz in range(1, depth):
        send(
            kv.at[z, a],
            kv.at[z, a],
            kv_send.at[n_kv],
            kv_recv.at[z, a],
            ((z + dz) % depth * INNER + a, g),
        )
        n_kv += 1

    def columns(ga, aa, part):
        start = (ga * INNER + aa) * cols + part * half
        return pl.ds(pl.multiple_of(start, half), half)

    own = [
        pltpu.make_async_copy(
            w_ref.at[0, :, columns(g, a, part)], wbuf.at[part, z, g, a], own_sem.at[part]
        )
        for part in range(halves)
    ]
    n_w = 0
    for part in range(halves):
        own[part].start()
        for dg in range(groups):
            for da in range(INNER):
                if dg == 0 and da == 0:
                    continue
                gg = (g + dg) % groups
                aa = (a + da) % INNER
                send(
                    w_ref.at[0, :, columns(gg, aa, part)],
                    wbuf.at[part, z, g, a],
                    w_send.at[n_w],
                    w_recv.at[part, g, a],
                    (z * INNER + aa, gg),
                )
                n_w += 1

    def pass_on(block, part, to, exists, way, hop):
        copy = pltpu.make_async_remote_copy(
            src_ref=wbuf.at[part, block],
            dst_ref=wbuf.at[part, block],
            send_sem=wz_send.at[way, hop, part],
            recv_sem=wz_recv.at[block, part],
            device_id=(to * INNER + a, g),
            device_id_type=MESH,
        )
        pending_if.append((exists, copy))
        return copy

    def below_above(hop, part):
        below = z - hop
        above = z + hop
        for block, to, way in ((below, z + 1, 0), (above, z - 1, 1)):
            here = block >= 0 if way == 0 else block < depth
            onward = to < depth if way == 0 else to >= 0
            at = lax.clamp(0, block, depth - 1)
            exists = jnp.logical_and(here, onward)
            if hop:

                @pl.when(here)
                def _():
                    arrived(wbuf.at[part, at], wz_send.at[0, 0, 0], wz_recv.at[at, part])

            if hop < depth - 1:
                copy = pass_on(at, part, lax.clamp(0, to, depth - 1), exists, way, hop)

                @pl.when(exists)
                def _():
                    copy.start()

    def begin(part):
        own[part].wait()
        for dg in range(groups):
            gg = (g + dg) % groups
            for da in range(INNER):
                if dg == 0 and da == 0:
                    continue
                aa = (a + da) % INNER
                arrived(wbuf.at[part, z, gg, aa], w_send.at[0], w_recv.at[part, gg, aa])
        below_above(0, part)

    begin(0)

    for dz in range(depth):
        zz = (z + dz) % depth
        if dz:
            arrived(kv.at[zz, a], kv_send.at[0], kv_recv.at[zz, a])
        for aa in (a_x, a_c):
            send(
                kv.at[zz, a],
                kv.at[zz, a],
                kv_send.at[n_kv],
                kv_recv.at[zz, a],
                (z * INNER + aa, g),
            )
            n_kv += 1

    for part in range(1, halves):
        begin(part)

    for copy in brought[2:]:
        copy.wait()

    def spread(row):
        wide = jnp.broadcast_to(
            bounds_ref[row : row + 1, :].astype(jnp.float32), (V_DEV, tokens)
        )
        return wide.T

    low = spread(0)
    high = spread(1)
    for block in range(frames):
        allowed = (low <= block) & (high > block)
        bias[:, block * V_DEV : (block + 1) * V_DEV] = jnp.where(allowed, 0.0, very_low)

    for dz in range(depth):
        zz = (z + dz) % depth
        arrived(kv.at[zz, a_x], kv_send.at[0], kv_recv.at[zz, a_x])
        send(
            kv.at[zz, a_x],
            kv.at[zz, a_x],
            kv_send.at[n_kv],
            kv_recv.at[zz, a_x],
            (z * INNER + a_c, g),
        )
        n_kv += 1
    for dz in range(depth):
        zz = (z + dz) % depth
        for aa in (a_c, a_xc):
            arrived(kv.at[zz, aa], kv_send.at[0], kv_recv.at[zz, aa])

    fold = math.log2(math.e) / math.sqrt(HEAD_WIDTH)
    per = heads // parts
    rows = per * tokens
    pair = 2 * V_DEV

    def attend(part):
        normed = []
        for h in range(part * per, (part + 1) * per):
            x = q_ref[:, h * HEAD_WIDTH : (h + 1) * HEAD_WIDTH].astype(jnp.float32)
            x = x * lax.rsqrt(jnp.mean(x * x, axis=-1, keepdims=True) + 1e-05) * gain_ref[...]
            normed.append(x.astype(jnp.bfloat16))
        x = jnp.concatenate(normed, axis=0)
        top = jnp.full((rows, V_DEV), very_low, jnp.float32)
        for n in range(frames // 2):
            at = n * 2 // INNER
            first = n * 2 % INNER
            keys = kv[at, first : first + 2, 0].reshape(pair, HEAD_WIDTH)
            scores = lax.dot_general(
                x, keys, (((1,), (1,)), ((), ())), preferred_element_type=jnp.float32
            )
            offset = bias[:, n * pair : (n + 1) * pair]
            scores = scores * fold + jnp.concatenate([offset] * per, axis=0)
            logits[:, n * pair : (n + 1) * pair] = scores
            top = jnp.maximum(top, jnp.maximum(scores[:, :V_DEV], scores[:, V_DEV:]))
        top = jnp.max(top, axis=1, keepdims=True)
        total = jnp.zeros((rows, V_DEV), jnp.float32)
        summed = jnp.zeros((rows, HEAD_WIDTH), jnp.float32)
        for n in range(frames // 2):
            at = n * 2 // INNER
            first = n * 2 % INNER
            vals = kv[at, first : first + 2, 1].reshape(pair, HEAD_WIDTH)
            weights = jnp.exp2(logits[:, n * pair : (n + 1) * pair] - top)
            total = total + (weights[:, :V_DEV] + weights[:, V_DEV:])
            summed = summed + jnp.dot(
                weights.astype(jnp.bfloat16), vals, preferred_element_type=jnp.float32
            )
        total = jnp.sum(total, axis=1, keepdims=True)
        result = (summed / total).astype(jnp.bfloat16)
        for h in range(per):
            att[part, a, g, :, h * HEAD_WIDTH : (h + 1) * HEAD_WIDTH] = result[
                h * tokens : (h + 1) * tokens
            ]

    n_att = [0]

    def hand(part, aa, gg, to):
        send(
            att.at[part, aa, gg],
            att.at[part, aa, gg],
            att_send.at[n_att[0]],
            att_recv.at[part, aa, gg],
            to,
        )
        n_att[0] += 1

    def await_att(part, aa, gg):
        arrived(att.at[part, aa, gg], att_send.at[0], att_recv.at[part, aa, gg])

    tasks = [(hop, part) for hop in range(1, depth - 1) for part in range(halves)]
    steps = parts + 2
    for step in range(steps):
        if step < parts:
            attend(step)
        for hop, part in tasks[-(-step * len(tasks) // steps) : -(-(step + 1) * len(tasks) // steps)]:
            below_above(hop, part)
        if step < parts:
            for dg in range(1, groups):
                hand(step, a, g, (f, (g + dg) % groups))
            for aa in (a_x, a_c):
                hand(step, a, g, (z * INNER + aa, g))
        if 1 <= step <= parts:
            for dg in range(1, groups):
                gg = (g + dg) % groups
                await_att(step - 1, a, gg)
                for aa in (a_x, a_c):
                    hand(step - 1, a, gg, (z * INNER + aa, g))
        if step >= 2:
            for dg in range(groups):
                gg = (g + dg) % groups
                await_att(step - 2, a_x, gg)
                hand(step - 2, a_x, gg, (z * INNER + a_c, g))
    for part in range(parts):
        for dg in range(groups):
            gg = (g + dg) % groups
            for aa in (a_c, a_xc):
                await_att(part, aa, gg)

    gate = jnp.tanh(gate_ref[...])
    width = heads * HEAD_WIDTH

    def target(aa, part):
        return pl.ds(pl.multiple_of(aa * cols + part * half, half), half)

    for part in range(halves):
        below_above(depth - 1, part)
        acc = jnp.zeros((INNER * tokens, half), jnp.float32)
        for gg in range(groups):
            weight = wbuf[part, :, gg].reshape(width, half)
            for p in range(parts):
                acc = acc + jnp.dot(
                    att[p, :, gg].reshape(INNER * tokens, width // parts),
                    weight[p * (width // parts) : (p + 1) * (width // parts)],
                    preferred_element_type=jnp.float32,
                )
        done = (gate * acc).astype(jnp.bfloat16)
        obuf[part] = done.reshape(INNER, tokens, half)
        for da in (2, 3, 1):
            aa = (a + da) % INNER
            send(
                obuf.at[part, aa],
                out_ref.at[:, target(a, part)],
                out_send.at[part, da - 1],
                out_recv.at[part, a],
                (z * INNER + aa, g),
            )
        out_ref[:, target(a, part)] = obuf[part, a]
    for part in range(halves):
        for da in range(1, INNER):
            aa = (a + da) % INNER
            arrived(out_ref.at[:, target(aa, part)], out_send.at[0, 0], out_recv.at[part, aa])
    for copy in pending:
        copy.wait_send()
    for exists, copy in pending_if:

        @pl.when(exists)
        def _():
            copy.wait_send()


def local(queries, keys, values, q_gain, frame_bounds, output_weight, attn_gate):
    frames = lax.axis_size("frame")
    groups = lax.axis_size("group")
    tokens, width = queries.shape
    rows = output_weight.shape[1]
    cols = output_weight.shape[2] // (groups * INNER)
    depth = frames // INNER
    dma = pltpu.SemaphoreType.DMA
    vmem = pl.BlockSpec(memory_space=pltpu.VMEM)
    plane = groups * INNER
    heads = width // HEAD_WIDTH
    parts = 4
    per = heads // parts
    halves = cols // 128
    half = cols // halves
    anywhere = pl.BlockSpec(memory_space=pl.ANY)
    return pl.pallas_call(
        functools.partial(kernel, frames, groups),
        out_shape=jax.ShapeDtypeStruct((tokens, INNER * cols), jnp.bfloat16),
        in_specs=[anywhere] * 6 + [vmem],
        out_specs=vmem,
        scratch_shapes=[
            pltpu.VMEM((tokens, width), jnp.bfloat16),
            pltpu.VMEM((1, HEAD_WIDTH), jnp.float32),
            pltpu.VMEM((2, tokens), jnp.int32),
            pltpu.VMEM((tokens, frames * V_DEV), jnp.float32),
            pltpu.VMEM((per * tokens, frames * V_DEV), jnp.float32),
            pltpu.VMEM((depth, INNER, 2, keys.shape[0], HEAD_WIDTH), jnp.bfloat16),
            pltpu.VMEM((parts, INNER, groups, tokens, width // parts), jnp.bfloat16),
            pltpu.VMEM((halves, depth, groups, INNER, rows, half), jnp.bfloat16),
            pltpu.VMEM((halves, INNER, tokens, half), jnp.bfloat16),
            dma((depth, INNER)),
            dma((4 * depth - 1,)),
            dma((halves, groups, INNER)),
            dma((halves * (plane - 1),)),
            dma((depth, halves)),
            dma((2, depth - 1, halves)),
            dma((parts, INNER, groups)),
            dma((parts * (4 * groups - 1),)),
            dma((halves, INNER)),
            dma((halves, INNER - 1)),
            dma((halves,)),
            dma((5,)),
        ],
        compiler_params=pltpu.CompilerParams(
            collective_id=0, has_side_effects=True, vmem_limit_bytes=60 * 1024 * 1024
        ),
        cost_estimate=pl.CostEstimate(
            flops=3 * 1024**3, bytes_accessed=4 * 1024**2, transcendentals=2 * 1024**2
        ),
    )(
        queries,
        keys,
        values,
        q_gain.reshape(1, HEAD_WIDTH),
        frame_bounds,
        output_weight,
        attn_gate.reshape(1, 1),
    )


def solution(mesh):
    placed = (
        P("frame", "group"),
        P("frame", "group"),
        P("frame", "group"),
        P(),
        P(None, "frame"),
        P("group", "frame", None),
        P(),
    )
    return jax.shard_map(
        local, mesh=mesh, in_specs=placed, out_specs=P("frame", "group"), check_vma=False
    )
```
